256 devices in a mesh: frame: 16 (over x_lo, z), patch: 16 (over x_hi, y, core).
Axes of the slice: x: 4 (x_hi: 2, x_lo: 2; x = x_hi * 2 + x_lo), y: 4, z: 8, core: 2. Of those that a mesh axis runs over, the one named last changes fastest.
Arguments:
- frames_in: bfloat16 [512, 256, 1408], P('frame', 'patch'), may hold values from -8 to 8
- ln_gain: float32 [1408], replicated, may hold values from 0.25 to 1.75
- w_query: bfloat16 [1408, 704], replicated, may hold values from -1 to 1
- w_key: bfloat16 [1408, 704], replicated, may hold values from -4 to 4
- w_value: bfloat16 [1408, 704], replicated, may hold values from -0.15625 to 0.15625
- w_out: bfloat16 [704, 1408], replicated, may hold values from -0.21875 to 0.21875
- w_down: bfloat16 [1408, 352], replicated, may hold values from -0.15625 to 0.15625
- conv_kernel: float32 [3, 352], replicated, may hold values from -3 to 3
- w_up: bfloat16 [352, 1408], replicated, may hold values from -0.3125 to 0.3125
Outputs:
- adapted: bfloat16 [512, 256, 1408], P('frame', 'patch')
- pooled: float32 [512, 1408], P('frame', 'patch')
The draws below stay inside these ranges and needn't reach their ends.
All inputs are finite; a program needn't handle non-finite values.
Results may differ from the reference program's by a relative error of at most 0.017.
Values may be sent and summed in bfloat16 or wider, within the bound.
A program may use at most 192 MiB of HBM per device.

```python
import math
import jax
import jax.numpy as jnp
from jax import lax

D = 1408
HEADS = 8
HEAD_SIZE = 88
ADAPT = 352
HD = 704
FRAMES = 512
PATCHES = 256


def shared_base(key):
    base = jax.random.normal(key, (D, HD), jnp.float32)
    return jnp.clip(base, -6.0, 6.0) * D ** (-0.5)


def draw_frames_in(key, part):
    key = jax.random.fold_in(key, 11)
    first, second = jax.random.split(key, 2)
    common = jax.random.normal(second, (FRAMES, 1, D), jnp.float32)
    noise = jax.random.normal(first, (FRAMES, PATCHES, D), jnp.float32)
    tokens = noise + common
    return jnp.clip(tokens, -8.0, 8.0).astype(jnp.bfloat16)


def draw_w_query(key, part):
    return shared_base(key).astype(jnp.bfloat16)


def draw_w_key(key, part):
    key = jax.random.fold_in(key, 5)
    own = jnp.clip(jax.random.normal(key, (D, HD), jnp.float32), -6.0, 6.0) * D ** (-0.5)
    return own.astype(jnp.bfloat16)


def normal_values(own_key, shape, deviation, bound, held_as=jnp.bfloat16):
    return jnp.clip(deviation * jax.random.normal(own_key, shape, jnp.float32), -bound, bound).astype(held_as)


def setup_inputs(seed: int = 0) -> dict:
    key_list = jax.random.split(jax.random.key(seed), 10)
    return {
        "frames_in": draw_frames_in(jax.random.fold_in(key_list[9], 71), 0),
        "ln_gain": jnp.clip(1.0 + 0.15 * jax.random.normal(key_list[1], (D,), jnp.float32), 0.25, 1.75),
        "w_query": draw_w_query(jax.random.fold_in(key_list[9], 71), 0),
        "w_key": draw_w_key(jax.random.fold_in(key_list[9], 71), 0),
        "w_value": normal_values(key_list[4], (D, HD), D ** -0.5, 0.15625),
        "w_out": normal_values(key_list[5], (HD, D), HD ** -0.5, 0.21875),
        "w_down": normal_values(key_list[6], (D, ADAPT), D ** -0.5, 0.15625),
        "conv_kernel": normal_values(key_list[7], (3, ADAPT), 0.6, 3.0, jnp.float32),
        "w_up": normal_values(key_list[8], (ADAPT, D), ADAPT ** -0.5, 0.3125),
    }


def attend(queries, key_rows, value_rows):
    temper = 1.0 / math.sqrt(HEAD_SIZE)
    scores = jnp.einsum('fphe,fnhe->fhpn', queries.astype(jnp.float32), key_rows.astype(jnp.float32)) * temper
    top = lax.optimization_barrier(jnp.max(scores, axis=-1, keepdims=True))
    raised = jnp.exp(scores - top)
    totals = lax.optimization_barrier(jnp.sum(raised, axis=-1, keepdims=True))
    weights = raised.astype(jnp.bfloat16)
    summed = jnp.einsum('fhpn,fnhe->fphe', weights.astype(jnp.float32), value_rows.astype(jnp.float32))
    return (summed / jnp.transpose(totals, (0, 2, 1, 3))).astype(jnp.bfloat16)

def reference(frames_in, ln_gain, w_query, w_key, w_value, w_out, w_down, conv_kernel, w_up):

    def frame_block(tokens):
        wide = tokens.astype(jnp.float32)
        average = lax.optimization_barrier(jnp.mean(wide, axis=-1, keepdims=True))
        variance = lax.optimization_barrier(jnp.mean((wide - average) ** 2, axis=-1, keepdims=True))
        normed = ((wide - average) * lax.rsqrt(variance + 1e-06) * ln_gain).astype(jnp.bfloat16)
        shape_heads = (1, PATCHES, HEADS, HEAD_SIZE)
        queries = jnp.dot(normed, w_query, preferred_element_type=jnp.float32).astype(jnp.bfloat16).reshape(shape_heads)
        key_rows = jnp.dot(normed, w_key, preferred_element_type=jnp.float32).astype(jnp.bfloat16).reshape(shape_heads)
        value_rows = jnp.dot(normed, w_value, preferred_element_type=jnp.float32).astype(jnp.bfloat16).reshape(shape_heads)
        attended = attend(queries, key_rows, value_rows).reshape(PATCHES, HD)
        block_out = wide + jnp.dot(attended, w_out, preferred_element_type=jnp.float32)
        reduced = jnp.dot(block_out.astype(jnp.bfloat16), w_down, preferred_element_type=jnp.float32).astype(jnp.bfloat16)
        return (block_out, reduced)
    block_out, reduced = lax.map(frame_block, frames_in)
    padded = jnp.pad(reduced, ((1, 1), (0, 0), (0, 0)))
    blended = padded[:-2] * conv_kernel[0] + padded[1:-1] * conv_kernel[1] + padded[2:] * conv_kernel[2]
    activated = jax.nn.gelu(blended, approximate=True).astype(jnp.bfloat16)
    lifted = jnp.dot(activated.reshape(FRAMES * PATCHES, ADAPT), w_up, preferred_element_type=jnp.float32)
    full_out = block_out + lifted.reshape(FRAMES, PATCHES, D)
    adapted = full_out.astype(jnp.bfloat16)
    pooled = lax.optimization_barrier(jnp.sum(full_out, axis=1)) / PATCHES
    return (adapted, pooled)
```

```python
import functools
import math

import jax
import jax.numpy as jnp
from jax import lax
from jax.experimental import pallas as pl
from jax.experimental.pallas import tpu as pltpu
from jax.sharding import PartitionSpec as P

HEAD_SIZE = 88
LANES = 128
MESH = pl.DeviceIdType.MESH
F32 = jnp.float32
BF16 = jnp.bfloat16


def dot(a, b):
    return jnp.dot(a, b, preferred_element_type=F32)


def dot_turned(a, b):
    return lax.dot_general(a, b, (((1,), (1,)), ((), ())), preferred_element_type=F32)


def layer_kernel(
    n, ring,
    x_ref, gain_ref, wq_ref, wk_ref, wv_ref, wo_ref, wd_ref, conv_ref, wu_ref,
    adapted_ref, pooled_ref,
    home, xr, normed, q, k, v, acc, att, ah, wq, wk, wv, wo, wd, wu,
    block, red, halo, part, psend, precv,
    load_sem, own_sem, x_send, x_recv, a_send, a_recv, h_send, h_recv, p_send, p_recv,
):
    f, p = lax.axis_index("frame"), lax.axis_index("patch")
    patches, width = x_ref.shape[1], x_ref.shape[2]
    features = wq.shape[0]
    tokens = n * patches
    half = n // 2
    quarter = half * patches

    def start_of(c, u):
        return c * half + u * ((n + half) * (1 - c) + half * c)

    def frame_of(c, j):
        u = j // half
        return start_of(c, u) + j - u * half

    loads = [
        pltpu.make_async_copy(src, dst, load_sem.at[i])
        for i, (src, dst) in enumerate(
            [(wq_ref, wq), (wk_ref, wk), (wv_ref, wv), (wo_ref, wo), (wd_ref, wd), (wu_ref, wu)]
        )
    ]

    def own_x(c):
        return pltpu.make_async_copy(x_ref.at[frame_of(c, p)], xr.at[c, p], own_sem.at[c])

    def own_att(c):
        return pltpu.make_async_copy(att.at[c, p], ah.at[c, p], own_sem.at[2 + c])

    def home_copy(c, u):
        return pltpu.make_async_copy(
            x_ref.at[pl.ds(start_of(c, u), half)],
            home.at[c, pl.ds(u * half, half)],
            own_sem.at[4 + 2 * c + u],
        )

    def x_copy(c, i):
        d = lax.rem(p + i, n)
        return pltpu.make_async_remote_copy(
            x_ref.at[frame_of(c, d)], xr.at[c, p], x_send.at[c, i], x_recv.at[c, p],
            device_id=(f, d), device_id_type=MESH,
        )

    def x_arrival(c, s):
        return pltpu.make_async_remote_copy(
            x_ref.at[0], xr.at[c, s], x_send.at[c, 0], x_recv.at[c, s],
            device_id=(f, s), device_id_type=MESH,
        )

    def a_copy(c, i):
        d = lax.rem(p + i, n)
        return pltpu.make_async_remote_copy(
            att.at[c, d], ah.at[c, p], a_send.at[c, i], a_recv.at[c, p],
            device_id=(f, d), device_id_type=MESH,
        )

    def a_arrival(c, s):
        return pltpu.make_async_remote_copy(
            att.at[c, 0], ah.at[c, s], a_send.at[c, 0], a_recv.at[c, s],
            device_id=(f, s), device_id_type=MESH,
        )

    before, after = lax.rem(f + ring - 1, ring), lax.rem(f + 1, ring)
    last = 2 * n
    to_after = pltpu.make_async_remote_copy(
        red.at[last], halo.at[0], h_send.at[0], h_recv.at[0],
        device_id=(after, p), device_id_type=MESH,
    )
    to_before = pltpu.make_async_remote_copy(
        red.at[1], halo.at[1], h_send.at[1], h_recv.at[1],
        device_id=(before, p), device_id_type=MESH,
    )

    def p_copy(i):
        d = lax.rem(p + i, n)
        return pltpu.make_async_remote_copy(
            psend.at[d], precv.at[p], p_send.at[i], p_recv.at[p],
            device_id=(f, d), device_id_type=MESH,
        )

    def p_arrival(s):
        return pltpu.make_async_remote_copy(
            psend.at[0], precv.at[s], p_send.at[0], p_recv.at[s],
            device_id=(f, s), device_id_type=MESH,
        )

    barrier = pltpu.get_barrier_semaphore()

    @pl.loop(1, n)
    def _(i):
        pl.semaphore_signal(barrier, inc=1, device_id=(f, lax.rem(p + i, n)), device_id_type=MESH)

    for side in (before, after):
        pl.semaphore_signal(barrier, inc=1, device_id=(side, p), device_id_type=MESH)

    own_x(0).start()
    for load in loads[:3]:
        load.start()
    own_x(1).start()
    for c in range(2):
        for u in range(2):
            home_copy(c, u).start()
    for load in loads[3:]:
        load.start()

    pl.semaphore_wait(barrier, n + 1)

    @pl.loop(1, n)
    def _(i):
        x_copy(0, i).start()

    def attention():
        lane = lax.broadcasted_iota(jnp.int32, (1, 2 * LANES), 1)
        scale = math.log2(math.e) / math.sqrt(HEAD_SIZE)
        for h in range(features // HEAD_SIZE):
            low = h * HEAD_SIZE
            a = low // LANES * LANES
            b = min(-(-(low + HEAD_SIZE) // LANES) * LANES, features)
            inside = (lane[:, : b - a] >= low - a) & (lane[:, : b - a] < low - a + HEAD_SIZE)
            mine = inside.astype(F32).astype(BF16)
            scores = dot_turned(q[:, a:b] * mine, k[:, a:b])
            top = jnp.max(scores, axis=-1, keepdims=True)
            raised = jnp.exp2((scores - top) * scale)
            totals = jnp.sum(raised, axis=-1, keepdims=True)
            summed = dot(raised.astype(BF16), v[:, a:b]) / totals
            acc[:, a:b] = jnp.where(inside, summed, acc[:, a:b])

    @pl.loop(0, 2)
    def _(c):
        @pl.loop(0, n)
        def _(i):
            s = lax.rem(p + n - i, n)

            @pl.when(i == 0)
            def _():
                own_x(c).wait()

            @pl.when(i > 0)
            def _():
                x_arrival(c, s).wait_recv()

                @pl.when(c == 0)
                def _():
                    x_copy(1, i).start()

            wide = xr[c, s].astype(F32)
            centered = wide - jnp.mean(wide, axis=-1, keepdims=True)
            variance = jnp.mean(centered * centered, axis=-1, keepdims=True)
            rows = pl.ds(pl.multiple_of(s * patches, patches), patches)
            normed[rows, :] = (centered * lax.rsqrt(variance + 1e-06) * gain_ref[...].reshape(1, width)).astype(BF16)

        @pl.when(c == 0)
        def _():
            for load in loads[:3]:
                load.wait()

        @pl.when(c == 1)
        def _():
            @pl.loop(1, n)
            def _(i):
                a_copy(0, i).start()

        for dst, weight in ((q, wq), (k, wk), (v, wv)):
            dst[...] = dot_turned(normed[...], weight[...]).astype(BF16)
        attention()
        att[c] = acc[...].astype(BF16).reshape(n, patches, features)
        own_att(c).start()

    @pl.loop(1, n)
    def _(i):
        a_copy(1, i).start()

    for load in loads[3:]:
        load.wait()

    @pl.loop(0, 2)
    def _(c):
        for u in range(2):
            home_copy(c, u).wait()
        own_att(c).wait()

        @pl.loop(1, n)
        def _(i):
            a_arrival(c, lax.rem(p + n - i, n)).wait_recv()

        here = dot(ah[c].reshape(tokens, features), wo[...])
        here += home[c].reshape(tokens, width).astype(F32)
        block[c] = here
        reduced = dot_turned(here.astype(BF16), wd[...]).astype(BF16)
        reduced = reduced.reshape(n, patches, wd.shape[0])
        for u in range(2):
            red[pl.ds(1 + start_of(c, u), half)] = reduced[u * half : (u + 1) * half]

        @pl.when(c == 0)
        def _():
            to_after.start()
            to_before.start()

    to_after.wait()
    to_before.wait()
    red[0] = jnp.where(f > 0, halo[0].astype(F32), 0.0).astype(BF16)
    red[last + 1] = jnp.where(f < ring - 1, halo[1].astype(F32), 0.0).astype(BF16)

    @pl.loop(0, 4)
    def _(j):
        c, u = j // 2, j % 2
        start = start_of(c, u)
        taps = [red[pl.ds(start + t, half)].astype(F32) * conv_ref[t : t + 1, :] for t in range(3)]
        activated = jax.nn.gelu(taps[0] + taps[1] + taps[2], approximate=True).astype(BF16)
        rows = pl.ds(pl.multiple_of(u * quarter, quarter), quarter)
        full = block[c, rows, :] + dot(activated.reshape(quarter, wu.shape[0]), wu[...])
        full = full.reshape(half, patches, width)
        part[pl.ds(pl.multiple_of(start, half), half), :] = jnp.sum(full, axis=1) / (n * patches)
        adapted_ref[pl.ds(start, half)] = full.astype(BF16)

    share = width // n
    for d in range(n):
        psend[d, :, :share] = part[:, d * share : (d + 1) * share].astype(BF16)

    @pl.loop(1, n)
    def _(i):
        p_copy(i).start()

    precv[p] = psend[p]

    @pl.loop(1, n)
    def _(i):
        p_arrival(lax.rem(p + n - i, n)).wait_recv()

    pooled_ref[...] = jnp.sum(precv[...].astype(F32), axis=0)[:, :share]

    @pl.loop(1, n)
    def _(i):
        for c in range(2):
            x_copy(c, i).wait_send()
            a_copy(c, i).wait_send()
        p_copy(i).wait_send()


def per_device(n, ring, frames_in, ln_gain, w_query, w_key, w_value, w_out, w_down, conv_kernel, w_up):
    frames, patches, width = frames_in.shape
    features, adapt = w_query.shape[1], w_down.shape[1]
    tokens = n * patches
    share = width // n
    any_spec = pl.BlockSpec(memory_space=pltpu.HBM)
    vmem_spec = pl.BlockSpec(memory_space=pltpu.VMEM)
    dma = pltpu.SemaphoreType.DMA
    padded = -(-share // LANES) * LANES
    return pl.pallas_call(
        functools.partial(layer_kernel, n, ring),
        out_shape=(
            jax.ShapeDtypeStruct((frames, patches, width), BF16),
            jax.ShapeDtypeStruct((frames, share), F32),
        ),
        in_specs=[any_spec, vmem_spec] + [any_spec] * 5 + [vmem_spec, any_spec],
        out_specs=(vmem_spec, vmem_spec),
        scratch_shapes=[
            pltpu.VMEM((2, n, patches, width), BF16),
            pltpu.VMEM((2, n, patches, width), BF16),
            pltpu.VMEM((tokens, width), BF16),
            pltpu.VMEM((tokens, features), BF16),
            pltpu.VMEM((tokens, features), BF16),
            pltpu.VMEM((tokens, features), BF16),
            pltpu.VMEM((tokens, features), F32),
            pltpu.VMEM((2, n, patches, features), BF16),
            pltpu.VMEM((2, n, patches, features), BF16),
            pltpu.VMEM(w_query.shape[::-1], BF16),
            pltpu.VMEM(w_key.shape[::-1], BF16),
            pltpu.VMEM(w_value.shape[::-1], BF16),
            pltpu.VMEM(w_out.shape, BF16),
            pltpu.VMEM(w_down.shape[::-1], BF16),
            pltpu.VMEM(w_up.shape, BF16),
            pltpu.VMEM((2, tokens, width), F32),
            pltpu.VMEM((frames + 2, patches, adapt), BF16),
            pltpu.VMEM((2, patches, adapt), BF16),
            pltpu.VMEM((frames, width), F32),
            pltpu.VMEM((n, frames, padded), BF16),
            pltpu.VMEM((n, frames, padded), BF16),
            dma((6,)), dma((8,)), dma((2, n)), dma((2, n)), dma((2, n)), dma((2, n)),
            dma((2,)), dma((2,)), dma((n,)), dma((n,)),
        ],
        compiler_params=pltpu.CompilerParams(
            collective_id=0, has_side_effects=True, vmem_limit_bytes=48 * 1024 * 1024
        ),
    )(
        frames_in, ln_gain, w_query.T, w_key.T, w_value.T, w_out, w_down.T, conv_kernel, w_up,
    )


def solution(mesh):
    placed = (P("frame", "patch", None), P(), P(), P(), P(), P(), P(), P(), P())
    return jax.shard_map(
        functools.partial(per_device, mesh.shape["patch"], mesh.shape["frame"]),
        mesh=mesh,
        in_specs=placed,
        out_specs=(P("frame", "patch", None), P("frame", "patch")),
        check_vma=False,
    )
```

```python
import functools
import math

import jax
import jax.numpy as jnp
from jax import lax
from jax.experimental import pallas as pl
from jax.experimental.pallas import tpu as pltpu
from jax.sharding import PartitionSpec as P

HEAD_SIZE = 88
SLOTS = 4
LANES = 128
MESH = pl.DeviceIdType.MESH
F32 = jnp.float32
BF16 = jnp.bfloat16


def dot(a, b):
    return jnp.dot(a, b, preferred_element_type=F32)


def dot_turned(a, b):
    return lax.dot_general(a, b, (((1,), (1,)), ((), ())), preferred_element_type=F32)


def layer_kernel(
    n, ring,
    x_ref, gain_ref, wq_ref, wk_ref, wv_ref, wo_ref, wd_ref, conv_ref, wu_ref,
    adapted_ref, pooled_ref,
    home, xr, normed, q, k, v, acc, att, ah, wq, wk, wv, wo, wd, wu,
    block, red, halo, part, psend, precv,
    load_sem, own_sem, x_send, x_recv, a_send, a_recv, h_send, h_recv, p_send, p_recv,
):
    f, p = lax.axis_index("frame"), lax.axis_index("patch")
    patches, width = x_ref.shape[1], x_ref.shape[2]
    features = wq.shape[0]
    tokens = n * patches
    half = n // 2

    def start_of(c, u):
        return c * half + u * ((n + half) * (1 - c) + half * c)

    def frame_of(c, j):
        u = j // half
        return start_of(c, u) + j - u * half

    loads = [
        pltpu.make_async_copy(src, dst, load_sem.at[i])
        for i, (src, dst) in enumerate(
            [(wq_ref, wq), (wk_ref, wk), (wv_ref, wv), (wo_ref, wo), (wd_ref, wd), (wu_ref, wu)]
        )
    ]

    def own_x(c):
        return pltpu.make_async_copy(home.at[frame_of(c, p)], xr.at[c, 0], own_sem.at[c])

    def own_att(c):
        return pltpu.make_async_copy(att.at[c, 0], ah.at[c, p], own_sem.at[2 + c])

    home_copy = pltpu.make_async_copy(x_ref, home, own_sem.at[4])

    def x_copy(c, i):
        d = lax.rem(p + i, n)
        return pltpu.make_async_remote_copy(
            home.at[frame_of(c, d)], xr.at[c, i], x_send.at[c, i], x_recv.at[c, i],
            device_id=(f, d), device_id_type=MESH,
        )

    def a_copy(c, i):
        d = lax.rem(p + n - i, n)
        return pltpu.make_async_remote_copy(
            att.at[c, i], ah.at[c, p], a_send.at[c, i], a_recv.at[c, p],
            device_id=(f, d), device_id_type=MESH,
        )

    def a_arrival(c, s):
        return pltpu.make_async_remote_copy(
            att.at[c, 0], ah.at[c, s], a_send.at[c, 0], a_recv.at[c, s],
            device_id=(f, s), device_id_type=MESH,
        )

    before, after = lax.rem(f + ring - 1, ring), lax.rem(f + 1, ring)
    last = 2 * n
    to_after = pltpu.make_async_remote_copy(
        red.at[last], halo.at[0], h_send.at[0], h_recv.at[0],
        device_id=(after, p), device_id_type=MESH,
    )
    to_before = pltpu.make_async_remote_copy(
        red.at[1], halo.at[1], h_send.at[1], h_recv.at[1],
        device_id=(before, p), device_id_type=MESH,
    )

    def p_copy(i):
        d = lax.rem(p + i, n)
        return pltpu.make_async_remote_copy(
            psend.at[d], precv.at[i], p_send.at[i], p_recv.at[i],
            device_id=(f, d), device_id_type=MESH,
        )

    home_copy.start()
    barrier = pltpu.get_barrier_semaphore()

    @pl.loop(1, n)
    def _(i):
        pl.semaphore_signal(barrier, inc=1, device_id=(f, lax.rem(p + i, n)), device_id_type=MESH)

    for side in (before, after):
        pl.semaphore_signal(barrier, inc=1, device_id=(side, p), device_id_type=MESH)

    for load in loads:
        load.start()
    home_copy.wait()
    for c in range(2):
        own_x(c).start()
    pl.semaphore_wait(barrier, n + 1)

    @pl.loop(1, n)
    def _(i):
        x_copy(0, i).start()

    @pl.loop(1, n)
    def _(i):
        x_copy(1, i).start()

    def attention():
        lane = lax.broadcasted_iota(jnp.int32, (1, 2 * LANES), 1)
        scale = math.log2(math.e) / math.sqrt(HEAD_SIZE)
        for h in range(features // HEAD_SIZE):
            low = h * HEAD_SIZE
            a = low // LANES * LANES
            b = min(-(-(low + HEAD_SIZE) // LANES) * LANES, features)
            inside = (lane[:, : b - a] >= low - a) & (lane[:, : b - a] < low - a + HEAD_SIZE)
            mine = inside.astype(F32).astype(BF16)
            scores = dot_turned(q[:, a:b] * mine, k[:, a:b])
            top = jnp.max(scores, axis=-1, keepdims=True)
            raised = jnp.exp2((scores - top) * scale)
            totals = jnp.sum(raised, axis=-1, keepdims=True)
            summed = dot(raised.astype(BF16), v[:, a:b]) / totals
            acc[:, a:b] = jnp.where(inside, summed, acc[:, a:b])

    rows_in = SLOTS * patches

    @pl.loop(0, 2)
    def _(c):
        @pl.loop(0, n // SLOTS)
        def _(g):
            for i in range(SLOTS):
                slot = g * SLOTS + i

                @pl.when(slot == 0)
                def _():
                    own_x(c).wait()

                @pl.when(slot > 0)
                def _():
                    x_copy(c, slot).wait_recv()

            wide = xr[c, pl.ds(g * SLOTS, SLOTS)].reshape(rows_in, width).astype(F32)
            centered = wide - jnp.mean(wide, axis=-1, keepdims=True)
            variance = jnp.mean(centered * centered, axis=-1, keepdims=True)
            gain = gain_ref[...].reshape(1, width)
            rows = pl.ds(pl.multiple_of(g * rows_in, rows_in), rows_in)
            normed[rows, :] = (centered * lax.rsqrt(variance + 1e-06) * gain).astype(BF16)

        @pl.when(c == 0)
        def _():
            for load in loads[:3]:
                load.wait()

        for dst, weight in ((q, wq), (k, wk), (v, wv)):
            dst[...] = dot_turned(normed[...], weight[...]).astype(BF16)
        attention()
        att[c] = acc[...].astype(BF16).reshape(n, patches, features)
        own_att(c).start()

        @pl.loop(1, n)
        def _(i):
            a_copy(c, i).start()

    for load in loads[3:]:
        load.wait()

    def come_home(c):
        own_att(c).wait()

        @pl.loop(1, n)
        def _(i):
            a_arrival(c, lax.rem(p + n - i, n)).wait_recv()

        here = dot(ah[c].reshape(tokens, features), wo[...])
        tokens_in = jnp.concatenate([home[start_of(c, u) : start_of(c, u) + half] for u in range(2)])
        here += tokens_in.reshape(tokens, width).astype(F32)
        reduced = dot_turned(here.astype(BF16), wd[...]).astype(BF16)
        here = here.reshape(n, patches, width)
        reduced = reduced.reshape(n, patches, wd.shape[0])
        for u in range(2):
            start = start_of(c, u)
            block[start : start + half] = here[u * half : (u + 1) * half]
            red[1 + start : 1 + start + half] = reduced[u * half : (u + 1) * half]

    def adapter(spans):
        taps = [
            jnp.concatenate([red[start + t : stop + t] for start, stop in spans]).astype(F32)
            * conv_ref[t : t + 1, :]
            for t in range(3)
        ]
        activated = jax.nn.gelu(taps[0] + taps[1] + taps[2], approximate=True).astype(BF16)
        count = activated.shape[0]
        lifted = dot(activated.reshape(count * patches, wu.shape[0]), wu[...])
        lifted = lifted.reshape(count, patches, width)
        at = 0
        for start, stop in spans:
            full = block[start:stop] + lifted[at : at + stop - start]
            part[start:stop, :] = jnp.sum(full, axis=1) / (n * patches)
            adapted_ref[start:stop] = full.astype(BF16)
            at += stop - start

    come_home(0)
    to_after.start()
    to_before.start()
    adapter([(1, half - 1), (last - half + 1, last - 1)])

    come_home(1)
    to_after.wait()
    to_before.wait()
    red[0] = jnp.where(f > 0, halo[0].astype(F32), 0.0).astype(BF16)
    red[last + 1] = jnp.where(f < ring - 1, halo[1].astype(F32), 0.0).astype(BF16)
    adapter([(0, 1), (half - 1, last - half + 1), (last - 1, last)])

    share = width // n
    for d in range(n):
        psend[d, :, :share] = part[:, d * share : (d + 1) * share].astype(BF16)

    @pl.loop(1, n)
    def _(i):
        p_copy(i).start()

    precv[0] = psend[p]

    @pl.loop(1, n)
    def _(i):
        for c in range(2):
            x_copy(c, i).wait_send()
            a_copy(c, i).wait_send()

    @pl.loop(1, n)
    def _(i):
        p_copy(i).wait_recv()

    pooled_ref[...] = jnp.sum(precv[...].astype(F32), axis=0)[:, :share]

    @pl.loop(1, n)
    def _(i):
        p_copy(i).wait_send()


def per_device(n, ring, frames_in, ln_gain, w_query, w_key, w_value, w_out, w_down, conv_kernel, w_up):
    frames, patches, width = frames_in.shape
    features, adapt = w_query.shape[1], w_down.shape[1]
    tokens = n * patches
    share = width // n
    any_spec = pl.BlockSpec(memory_space=pltpu.HBM)
    vmem_spec = pl.BlockSpec(memory_space=pltpu.VMEM)
    dma = pltpu.SemaphoreType.DMA
    padded = -(-share // LANES) * LANES
    return pl.pallas_call(
        functools.partial(layer_kernel, n, ring),
        out_shape=(
            jax.ShapeDtypeStruct((frames, patches, width), BF16),
            jax.ShapeDtypeStruct((frames, share), F32),
        ),
        in_specs=[any_spec, vmem_spec] + [any_spec] * 5 + [vmem_spec, any_spec],
        out_specs=(vmem_spec, vmem_spec),
        scratch_shapes=[
            pltpu.VMEM((frames, patches, width), BF16),
            pltpu.VMEM((2, n, patches, width), BF16),
            pltpu.VMEM((tokens, width), BF16),
            pltpu.VMEM((tokens, features), BF16),
            pltpu.VMEM((tokens, features), BF16),
            pltpu.VMEM((tokens, features), BF16),
            pltpu.VMEM((tokens, features), F32),
            pltpu.VMEM((2, n, patches, features), BF16),
            pltpu.VMEM((2, n, patches, features), BF16),
            pltpu.VMEM(w_query.shape[::-1], BF16),
            pltpu.VMEM(w_key.shape[::-1], BF16),
            pltpu.VMEM(w_value.shape[::-1], BF16),
            pltpu.VMEM(w_out.shape, BF16),
            pltpu.VMEM(w_down.shape[::-1], BF16),
            pltpu.VMEM(w_up.shape, BF16),
            pltpu.VMEM((frames, patches, width), F32),
            pltpu.VMEM((frames + 2, patches, adapt), BF16),
            pltpu.VMEM((2, patches, adapt), BF16),
            pltpu.VMEM((frames, width), F32),
            pltpu.VMEM((n, frames, padded), BF16),
            pltpu.VMEM((n, frames, padded), BF16),
            dma((6,)), dma((5,)), dma((2, n)), dma((2, n)), dma((2, n)), dma((2, n)),
            dma((2,)), dma((2,)), dma((n,)), dma((n,)),
        ],
        compiler_params=pltpu.CompilerParams(
            collective_id=0, has_side_effects=True, vmem_limit_bytes=60 * 1024 * 1024
        ),
    )(
        frames_in, ln_gain, w_query.T, w_key.T, w_value.T, w_out, w_down.T, conv_kernel, w_up,
    )


def solution(mesh):
    placed = (P("frame", "patch", None), P(), P(), P(), P(), P(), P(), P(), P())
    return jax.shard_map(
        functools.partial(per_device, mesh.shape["patch"], mesh.shape["frame"]),
        mesh=mesh,
        in_specs=placed,
        out_specs=(P("frame", "patch", None), P("frame", "patch")),
        check_vma=False,
    )
```

```python
import functools
import math

import jax
import jax.numpy as jnp
from jax import lax
from jax.experimental import pallas as pl
from jax.experimental.pallas import tpu as pltpu
from jax.sharding import PartitionSpec as P

HEAD_SIZE = 88
SLOTS = 4
PIECES = 4
LANES = 128
MESH = pl.DeviceIdType.MESH
F32 = jnp.float32
BF16 = jnp.bfloat16


def dot(a, b):
    return jnp.dot(a, b, preferred_element_type=F32)


def dot_turned(a, b):
    return lax.dot_general(a, b, (((1,), (1,)), ((), ())), preferred_element_type=F32)


def layer_kernel(
    n, ring,
    x_ref, gain_ref, wq_ref, wk_ref, wv_ref, wo_ref, wd_ref, conv_ref, wu_ref,
    adapted_ref, pooled_ref,
    home, xr, normed, q, k, v, acc, att, ah, wq, wk, wv, wo, wd, wu,
    block, red, halo, out, part, psend, precv,
    load_sem, own_sem, x_send, x_recv, a_send, a_recv, h_send, h_recv, p_send, p_recv, out_sem,
):
    f, p = lax.axis_index("frame"), lax.axis_index("patch")
    patches, width = x_ref.shape[1], x_ref.shape[2]
    features = wq.shape[0]
    tokens = n * patches
    half = n // 2

    def start_of(c, u):
        return c * half + u * ((n + half) * (1 - c) + half * c)

    def frame_of(c, j):
        u = j // half
        return start_of(c, u) + j - u * half

    loads = [
        pltpu.make_async_copy(src, dst, load_sem.at[i])
        for i, (src, dst) in enumerate(
            [(wq_ref, wq), (wk_ref, wk), (wv_ref, wv), (wo_ref, wo), (wd_ref, wd), (wu_ref, wu)]
        )
    ]

    def own_x(c):
        return pltpu.make_async_copy(home.at[frame_of(c, p)], xr.at[c, 0], own_sem.at[c])

    def own_att(c):
        return pltpu.make_async_copy(att.at[c, 0], ah.at[c, p], own_sem.at[2 + c])

    home_copy = pltpu.make_async_copy(x_ref, home, own_sem.at[4])

    def x_copy(c, i):
        d = lax.rem(p + 9 * i, n)
        return pltpu.make_async_remote_copy(
            home.at[frame_of(c, d)], xr.at[c, i], x_send.at[c, i], x_recv.at[c, i],
            device_id=(f, d), device_id_type=MESH,
        )

    def a_copy(c, i):
        d = lax.rem(p + 9 * (n - i), n)
        return pltpu.make_async_remote_copy(
            att.at[c, i], ah.at[c, p], a_send.at[c, i], a_recv.at[c, p],
            device_id=(f, d), device_id_type=MESH,
        )

    def a_arrival(c, s):
        return pltpu.make_async_remote_copy(
            att.at[c, 0], ah.at[c, s], a_send.at[c, 0], a_recv.at[c, s],
            device_id=(f, s), device_id_type=MESH,
        )

    before, after = lax.rem(f + ring - 1, ring), lax.rem(f + 1, ring)
    last = 2 * n
    to_after = pltpu.make_async_remote_copy(
        red.at[last], halo.at[0], h_send.at[0], h_recv.at[0],
        device_id=(after, p), device_id_type=MESH,
    )
    to_before = pltpu.make_async_remote_copy(
        red.at[1], halo.at[1], h_send.at[1], h_recv.at[1],
        device_id=(before, p), device_id_type=MESH,
    )

    def p_copy(i):
        d = lax.rem(p + 9 * i, n)
        return pltpu.make_async_remote_copy(
            psend.at[d], precv.at[i], p_send.at[i], p_recv.at[i],
            device_id=(f, d), device_id_type=MESH,
        )

    home_copy.start()
    barrier = pltpu.get_barrier_semaphore()

    @pl.loop(1, n)
    def _(i):
        pl.semaphore_signal(barrier, inc=1, device_id=(f, lax.rem(p + i, n)), device_id_type=MESH)

    for side in (before, after):
        pl.semaphore_signal(barrier, inc=1, device_id=(side, p), device_id_type=MESH)

    for load in loads:
        load.start()
    home_copy.wait()
    for c in range(2):
        own_x(c).start()
    pl.semaphore_wait(barrier, n + 1)

    @pl.loop(1, n)
    def _(i):
        x_copy(0, i).start()

    @pl.loop(1, n)
    def _(i):
        x_copy(1, i).start()

    def attention():
        lane = lax.broadcasted_iota(jnp.int32, (1, 2 * LANES), 1)
        scale = math.log2(math.e) / math.sqrt(HEAD_SIZE)
        for h in range(features // HEAD_SIZE):
            low = h * HEAD_SIZE
            a = low // LANES * LANES
            b = min(-(-(low + HEAD_SIZE) // LANES) * LANES, features)
            inside = (lane[:, : b - a] >= low - a) & (lane[:, : b - a] < low - a + HEAD_SIZE)
            mine = inside.astype(F32).astype(BF16)
            scores = dot_turned(q[:, a:b] * mine, k[:, a:b])
            top = jnp.max(scores, axis=-1, keepdims=True)
            raised = jnp.exp2((scores - top) * scale)
            totals = jnp.sum(raised, axis=-1, keepdims=True)
            summed = dot(raised.astype(BF16), v[:, a:b]) / totals
            acc[:, a:b] = jnp.where(inside, summed, acc[:, a:b])

    rows_in = SLOTS * patches

    @pl.loop(0, 2)
    def _(c):
        @pl.loop(0, n // SLOTS)
        def _(g):
            for i in range(SLOTS):
                slot = g * SLOTS + i

                @pl.when(slot == 0)
                def _():
                    own_x(c).wait()

                @pl.when(slot > 0)
                def _():
                    x_copy(c, slot).wait_recv()

            wide = xr[c, pl.ds(g * SLOTS, SLOTS)].reshape(rows_in, width).astype(F32)
            centered = wide - jnp.mean(wide, axis=-1, keepdims=True)
            variance = jnp.mean(centered * centered, axis=-1, keepdims=True)
            gain = gain_ref[...].reshape(1, width)
            rows = pl.ds(pl.multiple_of(g * rows_in, rows_in), rows_in)
            normed[rows, :] = (centered * lax.rsqrt(variance + 1e-06) * gain).astype(BF16)

        @pl.when(c == 0)
        def _():
            for load in loads[:3]:
                load.wait()

        for dst, weight in ((q, wq), (k, wk), (v, wv)):
            dst[...] = dot_turned(normed[...], weight[...]).astype(BF16)
        attention()
        att[c] = acc[...].astype(BF16).reshape(n, patches, features)
        own_att(c).start()

        @pl.loop(1, n)
        def _(i):
            a_copy(c, i).start()

    for load in loads[3:]:
        load.wait()

    def come_home(c):
        own_att(c).wait()

        @pl.loop(1, n)
        def _(i):
            a_arrival(c, lax.rem(p + n - i, n)).wait_recv()

        here = dot(ah[c].reshape(tokens, features), wo[...])
        tokens_in = jnp.concatenate([home[start_of(c, u) : start_of(c, u) + half] for u in range(2)])
        here += tokens_in.reshape(tokens, width).astype(F32)
        reduced = dot_turned(here.astype(BF16), wd[...]).astype(BF16)
        here = here.reshape(n, patches, width)
        reduced = reduced.reshape(n, patches, wd.shape[0])
        for u in range(2):
            start = start_of(c, u)
            block[start : start + half] = here[u * half : (u + 1) * half]
            red[1 + start : 1 + start + half] = reduced[u * half : (u + 1) * half]

    out_copies = []

    def adapter(spans):
        taps = [
            jnp.concatenate([red[start + t : stop + t] for start, stop in spans]).astype(F32)
            * conv_ref[t : t + 1, :]
            for t in range(3)
        ]
        activated = jax.nn.gelu(taps[0] + taps[1] + taps[2], approximate=True).astype(BF16)
        count = activated.shape[0]
        lifted = dot(activated.reshape(count * patches, wu.shape[0]), wu[...])
        lifted = lifted.reshape(count, patches, width)
        at = 0
        for start, stop in spans:
            full = block[start:stop] + lifted[at : at + stop - start]
            part[start:stop, :] = jnp.sum(full, axis=1) / (n * patches)
            out[start:stop] = full.astype(BF16)
            out_copies.append(pltpu.make_async_copy(out.at[start:stop], adapted_ref.at[start:stop], out_sem.at[len(out_copies)]))
            out_copies[-1].start()
            at += stop - start

    come_home(0)
    to_after.start()
    to_before.start()
    adapter([(1, half - 1), (last - half + 1, last - 1)])

    come_home(1)
    to_after.wait()
    to_before.wait()
    red[0] = jnp.where(f > 0, halo[0].astype(F32), 0.0).astype(BF16)
    red[last + 1] = jnp.where(f < ring - 1, halo[1].astype(F32), 0.0).astype(BF16)
    adapter([(0, 1), (half - 1, last - half + 1), (last - 1, last)])

    share = width // n
    for d in range(n):
        psend[d, :, :share] = part[:, d * share : (d + 1) * share].astype(BF16)

    @pl.loop(1, n)
    def _(i):
        p_copy(i).start()

    precv[0] = psend[p]

    @pl.loop(1, n)
    def _(i):
        for c in range(2):
            x_copy(c, i).wait_send()
            a_copy(c, i).wait_send()

    @pl.loop(1, n)
    def _(i):
        p_copy(i).wait_recv()

    for copy in out_copies:
        copy.wait()
    pooled_ref[...] = jnp.sum(precv[...].astype(F32), axis=0)[:, :share]

    @pl.loop(1, n)
    def _(i):
        p_copy(i).wait_send()


def deliver_kernel(rows_ref, sums_ref, rows_out, sums_out, held, held_sums, sems):
    step = rows_ref.shape[0] // PIECES
    pieces = [
        (rows_ref.at[pl.ds(i * step, step)], held.at[pl.ds(i * step, step)], rows_out.at[pl.ds(i * step, step)])
        for i in range(PIECES)
    ]
    pieces.append((sums_ref, held_sums, sums_out))
    reads = [pltpu.make_async_copy(a, b, sems.at[0, i]) for i, (a, b, _) in enumerate(pieces)]
    writes = [pltpu.make_async_copy(b, c, sems.at[1, i]) for i, (_, b, c) in enumerate(pieces)]
    for copy in reads:
        copy.start()
    for read, write in zip(reads, writes):
        read.wait()
        write.start()
    for copy in writes:
        copy.wait()


def deliver(rows, sums):
    anywhere = pl.BlockSpec(memory_space=pl.ANY)
    return pl.pallas_call(
        deliver_kernel,
        out_shape=(
            jax.ShapeDtypeStruct(rows.shape, rows.dtype),
            jax.ShapeDtypeStruct(sums.shape, sums.dtype),
        ),
        in_specs=[anywhere, anywhere],
        out_specs=(anywhere, anywhere),
        scratch_shapes=[
            pltpu.VMEM(rows.shape, rows.dtype),
            pltpu.VMEM(sums.shape, sums.dtype),
            pltpu.SemaphoreType.DMA((2, PIECES + 1)),
        ],
        compiler_params=pltpu.CompilerParams(vmem_limit_bytes=60 * 1024 * 1024),
    )(rows, sums)


def per_device(n, ring, frames_in, ln_gain, w_query, w_key, w_value, w_out, w_down, conv_kernel, w_up):
    frames, patches, width = frames_in.shape
    features, adapt = w_query.shape[1], w_down.shape[1]
    tokens = n * patches
    share = width // n
    any_spec = pl.BlockSpec(memory_space=pltpu.HBM)
    vmem_spec = pl.BlockSpec(memory_space=pltpu.VMEM)
    dma = pltpu.SemaphoreType.DMA
    padded = -(-share // LANES) * LANES
    rows, sums = pl.pallas_call(
        functools.partial(layer_kernel, n, ring),
        out_shape=(
            jax.ShapeDtypeStruct((frames, patches, width), BF16),
            jax.ShapeDtypeStruct((frames, share), F32),
        ),
        in_specs=[any_spec, vmem_spec] + [any_spec] * 5 + [vmem_spec, any_spec],
        out_specs=(any_spec, vmem_spec),
        scratch_shapes=[
            pltpu.VMEM((frames, patches, width), BF16),
            pltpu.VMEM((2, n, patches, width), BF16),
            pltpu.VMEM((tokens, width), BF16),
            pltpu.VMEM((tokens, features), BF16),
            pltpu.VMEM((tokens, features), BF16),
            pltpu.VMEM((tokens, features), BF16),
            pltpu.VMEM((tokens, features), F32),
            pltpu.VMEM((2, n, patches, features), BF16),
            pltpu.VMEM((2, n, patches, features), BF16),
            pltpu.VMEM(w_query.shape[::-1], BF16),
            pltpu.VMEM(w_key.shape[::-1], BF16),
            pltpu.VMEM(w_value.shape[::-1], BF16),
            pltpu.VMEM(w_out.shape, BF16),
            pltpu.VMEM(w_down.shape[::-1], BF16),
            pltpu.VMEM(w_up.shape, BF16),
            pltpu.VMEM((frames, patches, width), F32),
            pltpu.VMEM((frames + 2, patches, adapt), BF16),
            pltpu.VMEM((2, patches, adapt), BF16),
            pltpu.VMEM((frames, patches, width), BF16),
            pltpu.VMEM((frames, width), F32),
            pltpu.VMEM((n, frames, padded), BF16),
            pltpu.VMEM((n, frames, padded), BF16),
            dma((6,)), dma((5,)), dma((2, n)), dma((2, n)), dma((2, n)), dma((2, n)),
            dma((2,)), dma((2,)), dma((n,)), dma((n,)), dma((5,)),
        ],
        compiler_params=pltpu.CompilerParams(
            collective_id=0, has_side_effects=True, vmem_limit_bytes=60 * 1024 * 1024
        ),
    )(
        frames_in, ln_gain, w_query.T, w_key.T, w_value.T, w_out, w_down.T, conv_kernel, w_up,
    )
    return deliver(rows, sums)


def solution(mesh):
    placed = (P("frame", "patch", None), P(), P(), P(), P(), P(), P(), P(), P())
    return jax.shard_map(
        functools.partial(per_device, mesh.shape["patch"], mesh.shape["frame"]),
        mesh=mesh,
        in_specs=placed,
        out_specs=(P("frame", "patch", None), P("frame", "patch")),
        check_vma=False,
    )
```

```python
import functools
import math

import jax
import jax.numpy as jnp
from jax import lax
from jax.experimental import pallas as pl
from jax.experimental.pallas import tpu as pltpu
from jax.sharding import PartitionSpec as P

HEAD_SIZE = 88
SLOTS = 4
PIECES = 4
LANES = 128
MESH = pl.DeviceIdType.MESH
F32 = jnp.float32
BF16 = jnp.bfloat16


def dot(a, b):
    return jnp.dot(a, b, preferred_element_type=F32)


def dot_turned(a, b):
    return lax.dot_general(a, b, (((1,), (1,)), ((), ())), preferred_element_type=F32)


def layer_kernel(
    n, ring,
    x_ref, gain_ref, wq_ref, wk_ref, wv_ref, wo_ref, wd_ref, conv_ref, wu_ref,
    adapted_ref, pooled_ref,
    home, xr, normed, q, k, v, acc, att, ah, wq, wk, wv, wo, wd, wu,
    block, red, halo, out, part, psend, precv,
    load_sem, own_sem, x_send, x_recv, a_send, a_recv, h_send, h_recv, p_send, p_recv, out_sem,
):
    f, p = lax.axis_index("frame"), lax.axis_index("patch")
    patches, width = x_ref.shape[1], x_ref.shape[2]
    features = wq.shape[0]
    tokens = n * patches
    half = n // 2

    def start_of(c, u):
        return c * half + u * ((n + half) * (1 - c) + half * c)

    def frame_of(c, j):
        u = j // half
        return start_of(c, u) + j - u * half

    loads = [
        pltpu.make_async_copy(src, dst, load_sem.at[i])
        for i, (src, dst) in enumerate(
            [(wq_ref, wq), (wk_ref, wk), (wv_ref, wv), (wo_ref, wo), (wd_ref, wd), (wu_ref, wu)]
        )
    ]

    def own_x(c):
        return pltpu.make_async_copy(home.at[frame_of(c, p)], xr.at[c, 0], own_sem.at[c])

    def own_att(c):
        return pltpu.make_async_copy(att.at[c, 0], ah.at[c, p], own_sem.at[2 + c])

    home_copy = pltpu.make_async_copy(x_ref, home, own_sem.at[4])

    def x_copy(c, i):
        d = lax.rem(p + 9 * i, n)
        return pltpu.make_async_remote_copy(
            home.at[frame_of(c, d)], xr.at[c, i], x_send.at[c, i], x_recv.at[c, i],
            device_id=(f, d), device_id_type=MESH,
        )

    def a_copy(c, i):
        d = lax.rem(p + 9 * (n - i), n)
        return pltpu.make_async_remote_copy(
            att.at[c, i], ah.at[c, p], a_send.at[c, i], a_recv.at[c, p],
            device_id=(f, d), device_id_type=MESH,
        )

    def a_arrival(c, s):
        return pltpu.make_async_remote_copy(
            att.at[c, 0], ah.at[c, s], a_send.at[c, 0], a_recv.at[c, s],
            device_id=(f, s), device_id_type=MESH,
        )

    before, after = lax.rem(f + ring - 1, ring), lax.rem(f + 1, ring)
    last = 2 * n
    to_after = pltpu.make_async_remote_copy(
        red.at[last], halo.at[0], h_send.at[0], h_recv.at[0],
        device_id=(after, p), device_id_type=MESH,
    )
    to_before = pltpu.make_async_remote_copy(
        red.at[1], halo.at[1], h_send.at[1], h_recv.at[1],
        device_id=(before, p), device_id_type=MESH,
    )

    def p_copy(i):
        d = lax.rem(p + 9 * i, n)
        return pltpu.make_async_remote_copy(
            psend.at[d], precv.at[i], p_send.at[i], p_recv.at[i],
            device_id=(f, d), device_id_type=MESH,
        )

    home_copy.start()
    barrier = pltpu.get_barrier_semaphore()

    @pl.loop(1, n)
    def _(i):
        pl.semaphore_signal(barrier, inc=1, device_id=(f, lax.rem(p + i, n)), device_id_type=MESH)

    for side in (before, after):
        pl.semaphore_signal(barrier, inc=1, device_id=(side, p), device_id_type=MESH)

    for load in loads:
        load.start()
    home_copy.wait()
    for c in range(2):
        own_x(c).start()
    pl.semaphore_wait(barrier, n + 1)

    @pl.loop(1, n)
    def _(i):
        x_copy(0, i).start()

    @pl.loop(1, n)
    def _(i):
        x_copy(1, i).start()

    def attention():
        lane = lax.broadcasted_iota(jnp.int32, (1, 2 * LANES), 1)
        scale = math.log2(math.e) / math.sqrt(HEAD_SIZE)
        for h in range(features // HEAD_SIZE):
            low = h * HEAD_SIZE
            a = low // LANES * LANES
            b = min(-(-(low + HEAD_SIZE) // LANES) * LANES, features)
            inside = (lane[:, : b - a] >= low - a) & (lane[:, : b - a] < low - a + HEAD_SIZE)
            mine = inside.astype(F32).astype(BF16)
            scores = dot_turned(q[:, a:b] * mine, k[:, a:b])
            top = jnp.max(scores, axis=-1, keepdims=True)
            raised = jnp.exp2((scores - top) * scale)
            totals = jnp.sum(raised, axis=-1, keepdims=True)
            summed = dot(raised.astype(BF16), v[:, a:b]) / totals
            acc[:, a:b] = jnp.where(inside, summed, acc[:, a:b])

    rows_in = SLOTS * patches

    @pl.loop(0, 2)
    def _(c):
        @pl.loop(0, n // SLOTS)
        def _(g):
            for i in range(SLOTS):
                slot = g * SLOTS + i

                @pl.when(slot == 0)
                def _():
                    own_x(c).wait()

                @pl.when(slot > 0)
                def _():
                    x_copy(c, slot).wait_recv()

            wide = xr[c, pl.ds(g * SLOTS, SLOTS)].reshape(rows_in, width).astype(F32)
            centered = wide - jnp.mean(wide, axis=-1, keepdims=True)
            variance = jnp.mean(centered * centered, axis=-1, keepdims=True)
            gain = gain_ref[...].reshape(1, width)
            rows = pl.ds(pl.multiple_of(g * rows_in, rows_in), rows_in)
            normed[rows, :] = (centered * lax.rsqrt(variance + 1e-06) * gain).astype(BF16)

        @pl.when(c == 0)
        def _():
            for load in loads[:3]:
                load.wait()

        for dst, weight in ((q, wq), (k, wk), (v, wv)):
            dst[...] = dot_turned(normed[...], weight[...]).astype(BF16)
        attention()
        att[c] = acc[...].astype(BF16).reshape(n, patches, features)
        own_att(c).start()

        @pl.loop(1, n)
        def _(i):
            a_copy(c, n - i).start()

    for load in loads[3:]:
        load.wait()

    def come_home(c):
        own_att(c).wait()

        @pl.loop(1, n)
        def _(i):
            a_arrival(c, lax.rem(p + n - i, n)).wait_recv()

        here = dot(ah[c].reshape(tokens, features), wo[...])
        tokens_in = jnp.concatenate([home[start_of(c, u) : start_of(c, u) + half] for u in range(2)])
        here += tokens_in.reshape(tokens, width).astype(F32)
        reduced = dot_turned(here.astype(BF16), wd[...]).astype(BF16)
        here = here.reshape(n, patches, width)
        reduced = reduced.reshape(n, patches, wd.shape[0])
        for u in range(2):
            start = start_of(c, u)
            block[start : start + half] = here[u * half : (u + 1) * half]
            red[1 + start : 1 + start + half] = reduced[u * half : (u + 1) * half]

    out_copies = []

    def adapter(spans):
        taps = [
            jnp.concatenate([red[start + t : stop + t] for start, stop in spans]).astype(F32)
            * conv_ref[t : t + 1, :]
            for t in range(3)
        ]
        activated = jax.nn.gelu(taps[0] + taps[1] + taps[2], approximate=True).astype(BF16)
        count = activated.shape[0]
        lifted = dot(activated.reshape(count * patches, wu.shape[0]), wu[...])
        lifted = lifted.reshape(count, patches, width)
        at = 0
        for start, stop in spans:
            full = block[start:stop] + lifted[at : at + stop - start]
            part[start:stop, :] = jnp.sum(full, axis=1) / (n * patches)
            block[start:stop] = full
            at += stop - start

    def leave(spans):
        for start, stop in spans:
            out[start:stop] = block[start:stop].astype(BF16)
            copy = pltpu.make_async_copy(out.at[start:stop], adapted_ref.at[start:stop], out_sem.at[len(out_copies)])
            copy.start()
            out_copies.append(copy)

    early = [(1, half - 1), (last - half + 1, last - 1)]
    late = [(0, 1), (half - 1, last - half + 1), (last - 1, last)]

    come_home(0)
    to_after.start()
    to_before.start()
    adapter(early)
    leave(early)

    come_home(1)
    to_after.wait()
    to_before.wait()
    red[0] = jnp.where(f > 0, halo[0].astype(F32), 0.0).astype(BF16)
    red[last + 1] = jnp.where(f < ring - 1, halo[1].astype(F32), 0.0).astype(BF16)
    adapter(late)

    share = width // n
    for d in range(n):
        psend[d, :, :share] = part[:, d * share : (d + 1) * share].astype(BF16)

    @pl.loop(1, n)
    def _(i):
        p_copy(i).start()

    precv[0] = psend[p]
    leave(late)

    @pl.loop(1, n)
    def _(i):
        for c in range(2):
            x_copy(c, i).wait_send()
            a_copy(c, i).wait_send()

    @pl.loop(1, n)
    def _(i):
        p_copy(i).wait_recv()

    for copy in out_copies:
        copy.wait()
    pooled_ref[...] = jnp.sum(precv[...].astype(F32), axis=0)[:, :share]

    @pl.loop(1, n)
    def _(i):
        p_copy(i).wait_send()


def deliver_kernel(rows_ref, sums_ref, rows_out, sums_out, held, held_sums, sems):
    step = rows_ref.shape[0] // PIECES
    pieces = [
        (rows_ref.at[pl.ds(i * step, step)], held.at[pl.ds(i * step, step)], rows_out.at[pl.ds(i * step, step)])
        for i in range(PIECES)
    ]
    pieces.append((sums_ref, held_sums, sums_out))
    reads = [pltpu.make_async_copy(a, b, sems.at[0, i]) for i, (a, b, _) in enumerate(pieces)]
    writes = [pltpu.make_async_copy(b, c, sems.at[1, i]) for i, (_, b, c) in enumerate(pieces)]
    for copy in reads:
        copy.start()
    for read, write in zip(reads, writes):
        read.wait()
        write.start()
    for copy in writes:
        copy.wait()


def deliver(rows, sums):
    anywhere = pl.BlockSpec(memory_space=pl.ANY)
    return pl.pallas_call(
        deliver_kernel,
        out_shape=(
            jax.ShapeDtypeStruct(rows.shape, rows.dtype),
            jax.ShapeDtypeStruct(sums.shape, sums.dtype),
        ),
        in_specs=[anywhere, anywhere],
        out_specs=(anywhere, anywhere),
        scratch_shapes=[
            pltpu.VMEM(rows.shape, rows.dtype),
            pltpu.VMEM(sums.shape, sums.dtype),
            pltpu.SemaphoreType.DMA((2, PIECES + 1)),
        ],
        compiler_params=pltpu.CompilerParams(vmem_limit_bytes=60 * 1024 * 1024),
    )(rows, sums)


def per_device(n, ring, frames_in, ln_gain, w_query, w_key, w_value, w_out, w_down, conv_kernel, w_up):
    frames, patches, width = frames_in.shape
    features, adapt = w_query.shape[1], w_down.shape[1]
    tokens = n * patches
    share = width // n
    any_spec = pl.BlockSpec(memory_space=pltpu.HBM)
    vmem_spec = pl.BlockSpec(memory_space=pltpu.VMEM)
    dma = pltpu.SemaphoreType.DMA
    padded = -(-share // LANES) * LANES
    rows, sums = pl.pallas_call(
        functools.partial(layer_kernel, n, ring),
        out_shape=(
            jax.ShapeDtypeStruct((frames, patches, width), BF16),
            jax.ShapeDtypeStruct((frames, share), F32),
        ),
        in_specs=[any_spec, vmem_spec] + [any_spec] * 5 + [vmem_spec, any_spec],
        out_specs=(any_spec, vmem_spec),
        scratch_shapes=[
            pltpu.VMEM((frames, patches, width), BF16),
            pltpu.VMEM((2, n, patches, width), BF16),
            pltpu.VMEM((tokens, width), BF16),
            pltpu.VMEM((tokens, features), BF16),
            pltpu.VMEM((tokens, features), BF16),
            pltpu.VMEM((tokens, features), BF16),
            pltpu.VMEM((tokens, features), F32),
            pltpu.VMEM((2, n, patches, features), BF16),
            pltpu.VMEM((2, n, patches, features), BF16),
            pltpu.VMEM(w_query.shape[::-1], BF16),
            pltpu.VMEM(w_key.shape[::-1], BF16),
            pltpu.VMEM(w_value.shape[::-1], BF16),
            pltpu.VMEM(w_out.shape, BF16),
            pltpu.VMEM(w_down.shape[::-1], BF16),
            pltpu.VMEM(w_up.shape, BF16),
            pltpu.VMEM((frames, patches, width), F32),
            pltpu.VMEM((frames + 2, patches, adapt), BF16),
            pltpu.VMEM((2, patches, adapt), BF16),
            pltpu.VMEM((frames, patches, width), BF16),
            pltpu.VMEM((frames, width), F32),
            pltpu.VMEM((n, frames, padded), BF16),
            pltpu.VMEM((n, frames, padded), BF16),
            dma((6,)), dma((5,)), dma((2, n)), dma((2, n)), dma((2, n)), dma((2, n)),
            dma((2,)), dma((2,)), dma((n,)), dma((n,)), dma((5,)),
        ],
        compiler_params=pltpu.CompilerParams(
            collective_id=0, has_side_effects=True, vmem_limit_bytes=60 * 1024 * 1024
        ),
    )(
        frames_in, ln_gain, w_query.T, w_key.T, w_value.T, w_out, w_down.T, conv_kernel, w_up,
    )
    return deliver(rows, sums)


def solution(mesh):
    placed = (P("frame", "patch", None), P(), P(), P(), P(), P(), P(), P(), P())
    return jax.shard_map(
        functools.partial(per_device, mesh.shape["patch"], mesh.shape["frame"]),
        mesh=mesh,
        in_specs=placed,
        out_specs=(P("frame", "patch", None), P("frame", "patch")),
        check_vma=False,
    )
```
